512 devices in a mesh: rep: 16 (over x, z_lo), fsdp: 32 (over y, z_hi, core).
Axes of the slice: x: 4, y: 4, z: 16 (z_hi: 4, z_lo: 4; z = z_hi * 4 + z_lo), core: 2. Of those that a mesh axis runs over, the one named last changes fastest.
Arguments:
- inner_weights: bfloat16 [16, 512, 10240], P('rep', 'fsdp'), may hold values from -1000 to 1000
- master: float32 [512, 10240], P('fsdp'), may hold values from -6 to 6.5
- momentum: float32 [512, 10240], P('fsdp'), may hold values from -6 to 6
Outputs:
- new_master: float32 [512, 10240], P('fsdp')
- new_momentum: float32 [512, 10240], P('fsdp')
- working: bfloat16 [512, 10240], P('fsdp')
The draws below stay inside these ranges and needn't reach their ends.
All inputs are finite; a program needn't handle non-finite values.
Results may differ from the reference program's by a relative error of at most 0.0015.
Values may be sent and summed in bfloat16 or wider, within the bound.
No kernel may reach another device: no remote copies, remote signals or barrier semaphores. Data moves between devices by JAX's collectives and lax.ppermute only.
A program may use at most 64 MiB of HBM per device.

```python
import math
import jax
import jax.numpy as jnp
from jax import lax

COLS = 10240
ROWS = 512
REPLICAS = 16


def master_field(key):
    base = jax.random.normal(key, (ROWS, COLS), jnp.float32)
    return jnp.clip(base, -6.0, 6.0)


def log_range(key, count, lower, upper):
    return jnp.exp(jax.random.uniform(key, (count,), jnp.float32, math.log(lower), math.log(upper)))


def draw_master(key, part):
    return master_field(key)


def drift_field(key, upper, base_scale):
    row_ramp = 1.0 + 2.0 * jnp.arange(ROWS, dtype=jnp.float32) / ROWS
    col_ramp = 1.0 + 2.0 * jnp.arange(COLS, dtype=jnp.float32) / COLS
    row_scale = log_range(jax.random.fold_in(key, 21), ROWS, 1.0, upper) * row_ramp
    col_scale = log_range(jax.random.fold_in(key, 22), COLS, 1.0, upper) * col_ramp
    shared = jnp.clip(jax.random.normal(jax.random.fold_in(key, 23), (ROWS, COLS), jnp.float32), -4.0, 4.0)
    own_noise = jnp.clip(jax.random.normal(jax.random.fold_in(key, 24), (REPLICAS, ROWS, COLS), jnp.float32), -4.0, 4.0)
    replica_weight = log_range(jax.random.fold_in(key, 25), REPLICAS, 0.25, 2.0)
    column_noise = log_range(jax.random.fold_in(key, 26), COLS, 0.5, 2.0)
    scale = base_scale * row_scale[:, None] * col_scale[None, :]
    spread = replica_weight[:, None, None] * column_noise[None, None, :] * own_noise
    drawn = scale[None, :, :] * (shared[None, :, :] + spread)
    loud_count = max(1, COLS // 256)
    order = jax.random.permutation(jax.random.fold_in(key, 27), COLS)
    loud_flag = order < loud_count
    amplitude = log_range(jax.random.fold_in(key, 28), COLS, 1.0, 3.0)
    loud = 17.0 * row_ramp[None, :, None] * amplitude[None, None, :] * replica_weight[:, None, None] * jnp.clip(own_noise, -3.0, 3.0)
    return jnp.where(loud_flag[None, None, :], loud, drawn)


def draw_inner_weights(key, part):
    base = master_field(key)
    key = jax.random.fold_in(key, 2)
    drift = drift_field(key, 10.0, 0.03)
    return (base[None, :, :] + drift).astype(jnp.bfloat16)


def block_levels(own_key, extent, cuts, low, largest):
    gain, own = 1.0, jax.random.fold_in(own_key, 6)
    for axis_at, shards_of in cuts:
        steps = jnp.exp(jax.random.uniform(jax.random.fold_in(own, axis_at), (shards_of,), jnp.float32, low / len(cuts), largest / len(cuts)))
        gain = gain * jnp.repeat(steps, extent[axis_at] // shards_of).reshape([-1 if axis == axis_at else 1 for axis in range(len(extent))])
    return gain


def centred(stream_key, dims, width, bound, split=(), kind=jnp.bfloat16):
    drawn = width * jax.random.normal(stream_key, dims, jnp.float32)
    if split:
        drawn = drawn * block_levels(stream_key, dims, split, -0.22, 0.18)
    return jnp.clip(drawn, -bound, bound).astype(kind)


def setup_inputs(seed: int = 0) -> dict:
    streams_of = jax.random.split(jax.random.key(seed), 4)
    return {
        "inner_weights": draw_inner_weights(jax.random.fold_in(streams_of[3], 71), 0),
        "master": draw_master(jax.random.fold_in(streams_of[3], 71), 0),
        "momentum": centred(streams_of[2], (ROWS, COLS), 1.0, 6.0, ((0, 32),), jnp.float32),
    }


def reference(inner_weights, master, momentum):
    differences = master[None, :, :] - inner_weights.astype(jnp.float32)
    pseudo = lax.optimization_barrier(jnp.sum(differences, axis=0)) / REPLICAS
    squares = jnp.sum(pseudo * pseudo)
    factor = jnp.minimum(1.0, 0.5 * math.sqrt(ROWS * COLS) / jnp.sqrt(squares + 1e-06))
    clipped = factor * pseudo
    new_momentum = 0.9 * momentum + clipped
    new_master = master - 0.7 * (clipped + 0.9 * new_momentum)
    return (new_master, new_momentum, new_master.astype(jnp.bfloat16))
```

```python
import math

import jax
import jax.numpy as jnp
from jax import lax
from jax.sharding import PartitionSpec as P


def outer_step(pseudo, master, momentum, squares, element_count):
    factor = jnp.minimum(1.0, 0.5 * math.sqrt(element_count) / jnp.sqrt(squares + 1e-06))
    clipped = factor * pseudo
    new_momentum = 0.9 * momentum + clipped
    new_master = master - 0.7 * (clipped + 0.9 * new_momentum)
    return (new_master, new_momentum)


def to_all(piece, axis):
    copies = jnp.broadcast_to(piece[None], (lax.axis_size(axis),) + piece.shape)
    return lax.all_to_all(copies, axis, 0, 0, tiled=True)


def shards(inner_weights, master, momentum):
    replicas = lax.axis_size("rep")
    rows, cols = master.shape
    element_count = rows * lax.axis_size("fsdp") * cols
    bands = rows // 8
    across = replicas // bands
    width = cols // across
    pieces = inner_weights[0].reshape(bands, 8, across, width).transpose(0, 2, 1, 3).reshape(replicas, 8, width)
    received = lax.all_to_all(pieces, "rep", 0, 0, tiled=True)
    me = lax.axis_index("rep")
    own = lax.dynamic_slice(master, (me // across * 8, me % across * width), (8, width))
    summed = jnp.sum(own[None] - received.astype(jnp.float32), axis=0)
    gathered = to_all(summed / replicas, "rep")
    pseudo = gathered.reshape(bands, across, 8, width).transpose(0, 2, 1, 3).reshape(rows, cols)
    shares = to_all(jnp.full((128,), jnp.sum(pseudo * pseudo)), "fsdp")
    squares = jnp.sum(shares[:, 0])
    new_master, new_momentum = outer_step(pseudo, master, momentum, squares, element_count)
    return (new_master, new_momentum, new_master.astype(jnp.bfloat16))


def solution(mesh):
    placed = (P("rep", "fsdp", None), P("fsdp", None), P("fsdp", None))
    return jax.shard_map(
        shards,
        mesh=mesh,
        in_specs=placed,
        out_specs=(P("fsdp", None), P("fsdp", None), P("fsdp", None)),
        check_vma=False,
    )
```

```python
import math

import jax
import jax.numpy as jnp
from jax import lax
from jax.sharding import Mesh, PartitionSpec as P

SIZES = (4, 4, 4, 4, 2)
NAMES = ("x", "z_lo", "y", "z_hi", "core")
REP = ("x", "z_lo")
FSDP = ("y", "z_hi", "core")


def outer_step(pseudo, master, momentum, squares, element_count):
    factor = jnp.minimum(1.0, 0.5 * math.sqrt(element_count) / jnp.sqrt(squares + 1e-06))
    clipped = factor * pseudo
    new_momentum = 0.9 * momentum + clipped
    new_master = master - 0.7 * (clipped + 0.9 * new_momentum)
    return (new_master, new_momentum)


def position(x, z_lo, y, z_hi, core):
    place = 0
    for size, index in zip(SIZES, (x, z_lo, y, z_hi, core)):
        place = place * size + index
    return place


def near_groups():
    n_x, n_lo, n_y, n_hi, n_core = SIZES
    return [
        [
            position(x, (z_lo + n_lo // 2 * (z_hi * 2 // n_hi)) % n_lo, y, z_hi, core)
            for x in range(n_x)
            for y in range(n_y)
            for z_hi in range(n_hi)
            for core in range(n_core)
        ]
        for z_lo in range(n_lo)
    ]


def to_all(piece, size, axis, groups=None):
    copies = jnp.broadcast_to(piece[None], (size,) + piece.shape)
    return lax.all_to_all(copies, axis, 0, 0, axis_index_groups=groups, tiled=True)


def shards(inner_weights, master, momentum):
    replicas = lax.axis_size(REP)
    rows, cols = master.shape
    element_count = rows * lax.axis_size(FSDP) * cols
    bands = rows // 8
    across = replicas // bands
    width = cols // across
    pieces = inner_weights[0].reshape(bands, 8, across, width).transpose(0, 2, 1, 3).reshape(replicas, 8, width)
    received = lax.all_to_all(pieces, REP, 0, 0, tiled=True)
    me = lax.axis_index(REP)
    own = lax.dynamic_slice(master, (me // across * 8, me % across * width), (8, width))
    mean = jnp.sum(own[None] - received.astype(jnp.float32), axis=0) / replicas
    column = to_all(mean, lax.axis_size("z_lo"), "z_lo")
    groups = near_groups()
    shares = to_all(jnp.full((1, 128), jnp.sum(column * column)), len(groups[0]), NAMES, groups)
    gathered = lax.all_gather(column, "x")
    squares = jnp.sum(shares[:, 0, 0])
    pseudo = gathered.reshape(bands, across, 8, width).transpose(0, 2, 1, 3).reshape(rows, cols)
    new_master, new_momentum = outer_step(pseudo, master, momentum, squares, element_count)
    return (new_master, new_momentum, new_master.astype(jnp.bfloat16))


def solution(mesh):
    fine = Mesh(mesh.devices.reshape(SIZES), NAMES)
    rows = P(FSDP, None)
    return jax.shard_map(
        shards,
        mesh=fine,
        in_specs=(P(REP, FSDP, None), rows, rows),
        out_specs=(rows, rows, rows),
        check_vma=False,
    )
```

```python
import math

import jax
import jax.numpy as jnp
from jax import lax
from jax.experimental import pallas as pl
from jax.experimental.pallas import tpu as pltpu
from jax.sharding import Mesh, PartitionSpec as P

SIZES = (4, 4, 4, 4, 2)
NAMES = ("x", "z_lo", "y", "z_hi", "core")
REP = ("x", "z_lo")
FSDP = ("y", "z_hi", "core")
LANES = 128
SUBLANES = 8
OUT_CHUNKS = 4
PIECE_START = (2, 2)
SHARE_START = (0, 0, 3)


def turned(size, start):
    return [(start + step) % size for step in range(size)]


def position(x, z_lo, y, z_hi, core):
    place = 0
    for size, index in zip(SIZES, (x, z_lo, y, z_hi, core)):
        place = place * size + index
    return place


def near_groups():
    n_x, n_lo, n_y, n_hi, n_core = SIZES
    from_x, from_y, from_hi = SHARE_START
    return [
        [
            position(x, (z_lo + n_lo // 2 * (z_hi * 2 // n_hi)) % n_lo, y, z_hi, core)
            for x in turned(n_x, from_x)
            for y in turned(n_y, from_y)
            for z_hi in turned(n_hi, from_hi)
            for core in range(n_core)
        ]
        for z_lo in range(n_lo)
    ]


def squares_kernel(column_ref, shares_ref):
    pieces, _, width = column_ref.shape
    total = jnp.zeros((SUBLANES, LANES), jnp.float32)
    for piece in range(pieces):
        for start in range(0, width, LANES):
            value = column_ref[piece, :, start : start + LANES]
            total = total + value * value
    lanes = jnp.sum(total, axis=0, keepdims=True)
    shares_ref[...] = jnp.broadcast_to(lanes, shares_ref.shape)


def finish_kernel(
    element_count, shares_ref, pseudo_ref, master_ref, momentum_ref,
    new_master_ref, new_momentum_ref, working_ref,
    master_slot, momentum_slot, working_slot, sems,
):
    pieces, _, width = pseudo_ref.shape
    rows, cols = master_ref.shape
    bands = rows // SUBLANES
    across = pieces // bands
    squares = jnp.sum(shares_ref[...], keepdims=True)
    factor = jnp.minimum(1.0, 0.5 * math.sqrt(element_count) * lax.rsqrt(squares + 1e-06))
    copies = []
    chunk = cols // OUT_CHUNKS
    for block in range(across):
        at = slice(block * width, (block + 1) * width)
        pseudo = jnp.concatenate([pseudo_ref[band * across + block] for band in range(bands)], axis=0)
        clipped = factor * pseudo
        new_momentum = 0.9 * momentum_ref[:, at] + clipped
        new_master = master_ref[:, at] - 0.7 * (clipped + 0.9 * new_momentum)
        momentum_slot[:, at] = new_momentum
        master_slot[:, at] = new_master
        working_slot[:, at] = new_master.astype(jnp.bfloat16)
        done = (block + 1) * width
        if done % chunk == 0:
            part = slice(done - chunk, done)
            pairs = ((master_slot, new_master_ref), (momentum_slot, new_momentum_ref), (working_slot, working_ref))
            for k, (slot, out) in enumerate(pairs):
                copy = pltpu.make_async_copy(slot.at[:, part], out.at[:, part], sems.at[k, done // chunk - 1])
                copy.start()
                copies.append(copy)
    for copy in copies:
        copy.wait()


def shards(inner_weights, master, momentum):
    replicas = lax.axis_size(REP)
    rows, cols = master.shape
    element_count = rows * lax.axis_size(FSDP) * cols
    bands = rows // SUBLANES
    across = replicas // bands
    width = cols // across
    pieces = inner_weights[0].reshape(bands, SUBLANES, across, width).transpose(0, 2, 1, 3).reshape(replicas, SUBLANES, width)
    n_x, n_lo = lax.axis_size("x"), lax.axis_size("z_lo")
    from_x, from_lo = PIECE_START
    along_x, along_lo = turned(n_x, from_x), turned(n_lo, from_lo)
    along_rep = [x * n_lo + z_lo for x in along_x for z_lo in along_lo]
    received = lax.all_to_all(pieces, REP, 0, 0, axis_index_groups=[along_rep], tiled=True)
    me = (lax.axis_index("x") + n_x - from_x) % n_x * n_lo + (lax.axis_index("z_lo") + n_lo - from_lo) % n_lo
    own = lax.dynamic_slice(master, (me // across * SUBLANES, me % across * width), (SUBLANES, width))
    mean = jnp.sum(own[None] - received.astype(jnp.float32), axis=0) / replicas
    copies = jnp.broadcast_to(mean[None], (n_lo,) + mean.shape)
    column = lax.all_to_all(copies, "z_lo", 0, 0, axis_index_groups=[along_lo], tiled=True)
    groups = near_groups()
    members = len(groups[0])
    vmem = pl.BlockSpec(memory_space=pltpu.VMEM)
    shares = pl.pallas_call(
        squares_kernel,
        out_shape=jax.ShapeDtypeStruct((members, LANES), jnp.float32),
        in_specs=[vmem],
        out_specs=vmem,
        compiler_params=pltpu.CompilerParams(vmem_limit_bytes=4 << 20),
        cost_estimate=pl.CostEstimate(flops=2 * column.size, bytes_accessed=4 * column.size, transcendentals=0),
    )(column)
    shares = lax.all_to_all(shares.reshape(members, 1, LANES), NAMES, 0, 0, axis_index_groups=groups, tiled=True)
    gathered = lax.all_gather(column, "x", axis_index_groups=[along_x]).reshape(replicas, SUBLANES, width)
    whole = jax.ShapeDtypeStruct((rows, cols), jnp.float32)
    half = jax.ShapeDtypeStruct((rows, cols), jnp.bfloat16)
    hbm = pl.BlockSpec(memory_space=pl.ANY)
    return pl.pallas_call(
        lambda *refs: finish_kernel(element_count, *refs),
        out_shape=(whole, whole, half),
        in_specs=[vmem] * 4,
        out_specs=(hbm,) * 3,
        scratch_shapes=[
            pltpu.VMEM((rows, cols), jnp.float32),
            pltpu.VMEM((rows, cols), jnp.float32),
            pltpu.VMEM((rows, cols), jnp.bfloat16),
            pltpu.SemaphoreType.DMA((3, OUT_CHUNKS)),
        ],
        compiler_params=pltpu.CompilerParams(vmem_limit_bytes=16 << 20),
        cost_estimate=pl.CostEstimate(flops=8 * rows * cols, bytes_accessed=22 * rows * cols, transcendentals=0),
    )(shares.reshape(members, LANES), gathered, master, momentum)


def solution(mesh):
    fine = Mesh(mesh.devices.reshape(SIZES), NAMES)
    rows = P(FSDP, None)
    return jax.shard_map(
        shards,
        mesh=fine,
        in_specs=(P(REP, FSDP, None), rows, rows),
        out_specs=(rows, rows, rows),
        check_vma=False,
    )
```

```python
import math

import jax
import jax.numpy as jnp
from jax import lax
from jax.experimental import pallas as pl
from jax.experimental.pallas import tpu as pltpu
from jax.sharding import Mesh, PartitionSpec as P

SIZES = (4, 4, 4, 4, 2)
NAMES = ("x", "z_lo", "y", "z_hi", "core")
REP = ("x", "z_lo")
FSDP = ("y", "z_hi", "core")
LANES = 128
SUBLANES = 8
OUT_CHUNKS = 4
PIECE_START = (2, 2)
SHARE_START = (2, 3)
TOP = 14
FLOOR = 2.0**-100


def turned(size, start):
    return [(start + step) % size for step in range(size)]


def position(x, z_lo, y, z_hi, core):
    place = 0
    for size, index in zip(SIZES, (x, z_lo, y, z_hi, core)):
        place = place * size + index
    return place


def near_groups(pairs):
    n_x, n_lo, n_y, n_hi, n_core = SIZES
    from_y, from_hi = SHARE_START
    return [
        [
            position(x, (z_lo + n_lo // 2 * (z_hi * 2 // n_hi)) % n_lo, y, z_hi, core)
            for x in pair
            for y in turned(n_y, from_y)
            for z_hi in turned(n_hi, from_hi)
            for core in range(n_core)
        ]
        for pair in pairs
        for z_lo in range(n_lo)
    ]


def blocks(width):
    return [slice(start, start + LANES) for start in range(0, width, LANES)]


def encode(piece):
    parts = [piece[:, at] for at in blocks(piece.shape[1])]
    largest = jnp.full_like(parts[0], FLOOR)
    for part in parts:
        largest = jnp.maximum(largest, jnp.abs(part))
    exponent = jnp.ceil(jnp.log2(largest))
    power = jnp.exp2(TOP - exponent)
    return jnp.concatenate([part * power for part in parts] + [exponent], axis=1).astype(jnp.float16)


def power_of(coded_ref, piece, width):
    return jnp.exp2(coded_ref[piece, :, width : width + LANES] - TOP)


def squares_kernel(coded_ref, shares_ref):
    pieces, _, coded_width = coded_ref.shape
    width = coded_width - LANES
    total = jnp.zeros((SUBLANES, LANES), jnp.float32)
    for piece in range(pieces):
        power = power_of(coded_ref, piece, width)
        for at in blocks(width):
            value = coded_ref[piece, :, at] * power
            total = total + value * value
    lanes = jnp.sum(total, axis=0, keepdims=True)
    shares_ref[...] = jnp.broadcast_to(lanes, shares_ref.shape)


def finish_kernel(
    element_count, shares_ref, coded_ref, kept_ref, base_ref,
    new_master_ref, new_momentum_ref, working_ref,
    master_slot, momentum_slot, working_slot, sems,
):
    pieces, _, coded_width = coded_ref.shape
    width = coded_width - LANES
    rows, cols = kept_ref.shape
    bands = rows // SUBLANES
    across = pieces // bands
    squares = jnp.sum(shares_ref[...], keepdims=True)
    factor = jnp.minimum(1.0, 0.5 * math.sqrt(element_count) * lax.rsqrt(squares + 1e-06))
    copies = []
    chunk = cols // OUT_CHUNKS
    for block in range(across):
        own = [band * across + block for band in range(bands)]
        powers = [power_of(coded_ref, piece, width) for piece in own]
        for part in blocks(width):
            at = slice(block * width + part.start, block * width + part.stop)
            pseudo = jnp.concatenate([coded_ref[piece, :, part] * power for piece, power in zip(own, powers)], axis=0)
            clipped = factor * pseudo
            new_momentum = kept_ref[:, at] + clipped
            new_master = base_ref[:, at] - 1.33 * clipped
            momentum_slot[:, at] = new_momentum
            master_slot[:, at] = new_master
            working_slot[:, at] = new_master.astype(jnp.bfloat16)
        done = (block + 1) * width
        if done % chunk == 0:
            part = slice(done - chunk, done)
            pairs = ((master_slot, new_master_ref), (momentum_slot, new_momentum_ref), (working_slot, working_ref))
            for k, (slot, out) in enumerate(pairs):
                copy = pltpu.make_async_copy(slot.at[:, part], out.at[:, part], sems.at[k, done // chunk - 1])
                copy.start()
                copies.append(copy)
    for copy in copies:
        copy.wait()


def shards(inner_weights, master, momentum):
    replicas = lax.axis_size(REP)
    rows, cols = master.shape
    element_count = rows * lax.axis_size(FSDP) * cols
    bands = rows // SUBLANES
    across = replicas // bands
    width = cols // across
    pieces = inner_weights[0].reshape(bands, SUBLANES, across, width).transpose(0, 2, 1, 3).reshape(replicas, SUBLANES, width)
    n_x, n_lo = lax.axis_size("x"), lax.axis_size("z_lo")
    from_x, from_lo = PIECE_START
    along_x, along_lo = turned(n_x, from_x), turned(n_lo, from_lo)
    along_rep = [x * n_lo + z_lo for x in along_x for z_lo in along_lo]
    received = lax.all_to_all(pieces, REP, 0, 0, axis_index_groups=[along_rep], tiled=True)
    me = (lax.axis_index("x") + n_x - from_x) % n_x * n_lo + (lax.axis_index("z_lo") + n_lo - from_lo) % n_lo
    own = lax.dynamic_slice(master, (me // across * SUBLANES, me % across * width), (SUBLANES, width))
    mean = jnp.sum(own[None] - received.astype(jnp.float32), axis=0) / replicas
    kept = 0.9 * momentum
    base = master - 0.63 * kept
    mean, kept, base = lax.optimization_barrier((mean, kept, base))
    coded = encode(mean)
    near = replicas // bands
    copies = jnp.broadcast_to(coded[None], (near,) + coded.shape)
    firsts = [along_rep[start : start + near] for start in range(0, replicas, near)]
    band = lax.all_to_all(copies, REP, 0, 0, axis_index_groups=firsts, tiled=True)
    seconds = [[along_x[step], along_x[n_x - 1 - step]] for step in range(bands)]
    groups = near_groups(seconds)
    members = len(groups[0])
    vmem = pl.BlockSpec(memory_space=pltpu.VMEM)
    shares = pl.pallas_call(
        squares_kernel,
        out_shape=jax.ShapeDtypeStruct((members, LANES), jnp.float32),
        in_specs=[vmem],
        out_specs=vmem,
        compiler_params=pltpu.CompilerParams(vmem_limit_bytes=4 << 20),
        cost_estimate=pl.CostEstimate(flops=3 * band.size, bytes_accessed=4 * band.size, transcendentals=0),
    )(band.astype(jnp.float32))
    shares = lax.all_to_all(shares.reshape(members, 1, LANES), NAMES, 0, 0, axis_index_groups=groups, tiled=True)
    gathered = lax.all_gather(band, "x", axis_index_groups=seconds).reshape(replicas, SUBLANES, width + LANES).astype(jnp.float32)
    whole = jax.ShapeDtypeStruct((rows, cols), jnp.float32)
    half = jax.ShapeDtypeStruct((rows, cols), jnp.bfloat16)
    hbm = pl.BlockSpec(memory_space=pl.ANY)
    return pl.pallas_call(
        lambda *refs: finish_kernel(element_count, *refs),
        out_shape=(whole, whole, half),
        in_specs=[vmem] * 4,
        out_specs=(hbm,) * 3,
        scratch_shapes=[
            pltpu.VMEM((rows, cols), jnp.float32),
            pltpu.VMEM((rows, cols), jnp.float32),
            pltpu.VMEM((rows, cols), jnp.bfloat16),
            pltpu.SemaphoreType.DMA((3, OUT_CHUNKS)),
        ],
        compiler_params=pltpu.CompilerParams(vmem_limit_bytes=16 << 20),
        cost_estimate=pl.CostEstimate(flops=8 * rows * cols, bytes_accessed=22 * rows * cols, transcendentals=0),
    )(shares.reshape(members, LANES), gathered, kept, base)


def solution(mesh):
    fine = Mesh(mesh.devices.reshape(SIZES), NAMES)
    rows = P(FSDP, None)
    return jax.shard_map(
        shards,
        mesh=fine,
        in_specs=(P(REP, FSDP, None), rows, rows),
        out_specs=(rows, rows, rows),
        check_vma=False,
    )
```

```python
import math

import jax
import jax.numpy as jnp
from jax import lax
from jax.experimental import pallas as pl
from jax.experimental.pallas import tpu as pltpu
from jax.sharding import Mesh, PartitionSpec as P

SIZES = (4, 4, 4, 4, 2)
NAMES = ("x", "z_lo", "y", "z_hi", "core")
REP = ("x", "z_lo")
FSDP = ("y", "z_hi", "core")
LANES = 128
SUBLANES = 8
OUT_CHUNKS = 4
PIECE_START = (2, 2)
SHARE_START = (2, 3)
TOP = 14
FLOOR = 2.0**-100


def turned(size, start):
    return [(start + step) % size for step in range(size)]


def position(x, z_lo, y, z_hi, core):
    place = 0
    for size, index in zip(SIZES, (x, z_lo, y, z_hi, core)):
        place = place * size + index
    return place


def near_groups(pairs):
    n_x, n_lo, n_y, n_hi, n_core = SIZES
    from_y, from_hi = SHARE_START
    return [
        [
            position(x, (z_lo + n_lo // 2 * (z_hi * 2 // n_hi)) % n_lo, y, z_hi, core)
            for x in sorted(pair)
            for y in turned(n_y, from_y)
            for z_hi in turned(n_hi, from_hi)
            for core in range(n_core)
        ]
        for pair in pairs
        for z_lo in range(n_lo)
    ]


def blocks(width):
    return [slice(start, start + LANES) for start in range(0, width, LANES)]


def encode(piece):
    parts = [piece[:, at] for at in blocks(piece.shape[1])]
    largest = jnp.full_like(parts[0], FLOOR)
    for part in parts:
        largest = jnp.maximum(largest, jnp.abs(part))
    exponent = jnp.ceil(jnp.log2(largest))
    power = jnp.exp2(TOP - exponent)
    return jnp.concatenate([part * power for part in parts] + [exponent], axis=1).astype(jnp.float16)


def power_of(coded_ref, piece, width):
    return jnp.exp2(coded_ref[piece, :, width : width + LANES] - TOP)


def squares_kernel(coded_ref, shares_ref):
    pieces, _, coded_width = coded_ref.shape
    width = coded_width - LANES
    total = jnp.zeros((SUBLANES, LANES), jnp.float32)
    for piece in range(pieces):
        power = power_of(coded_ref, piece, width)
        for at in blocks(width):
            value = coded_ref[piece, :, at] * power
            total = total + value * value
    lanes = jnp.sum(total, axis=0, keepdims=True)
    shares_ref[...] = jnp.broadcast_to(lanes, shares_ref.shape)


def finish_kernel(
    element_count, shares_ref, coded_ref, kept_ref, base_ref,
    new_master_ref, new_momentum_ref, working_ref,
    master_slot, momentum_slot, working_slot, sems,
):
    pieces, _, coded_width = coded_ref.shape
    width = coded_width - LANES
    rows, cols = kept_ref.shape
    bands = rows // SUBLANES
    across = pieces // bands
    half = shares_ref.shape[0] // 2
    squares = jnp.sum(shares_ref[:half], keepdims=True) + jnp.sum(shares_ref[half:], keepdims=True)
    factor = jnp.minimum(1.0, 0.5 * math.sqrt(element_count) * lax.rsqrt(squares + 1e-06))
    copies = []
    chunk = cols // OUT_CHUNKS
    for block in range(across):
        own = [band * across + block for band in range(bands)]
        powers = [power_of(coded_ref, piece, width) for piece in own]
        for part in blocks(width):
            at = slice(block * width + part.start, block * width + part.stop)
            pseudo = jnp.concatenate([coded_ref[piece, :, part] * power for piece, power in zip(own, powers)], axis=0)
            clipped = factor * pseudo
            new_momentum = kept_ref[:, at] + clipped
            new_master = base_ref[:, at] - 1.33 * clipped
            momentum_slot[:, at] = new_momentum
            master_slot[:, at] = new_master
            working_slot[:, at] = new_master.astype(jnp.bfloat16)
        done = (block + 1) * width
        if done % chunk == 0:
            part = slice(done - chunk, done)
            pairs = ((master_slot, new_master_ref), (momentum_slot, new_momentum_ref), (working_slot, working_ref))
            for k, (slot, out) in enumerate(pairs):
                copy = pltpu.make_async_copy(slot.at[:, part], out.at[:, part], sems.at[k, done // chunk - 1])
                copy.start()
                copies.append(copy)
    for copy in copies:
        copy.wait()


def shards(inner_weights, master, momentum):
    replicas = lax.axis_size(REP)
    rows, cols = master.shape
    element_count = rows * lax.axis_size(FSDP) * cols
    bands = rows // SUBLANES
    across = replicas // bands
    width = cols // across
    pieces = inner_weights[0].reshape(bands, SUBLANES, across, width).transpose(0, 2, 1, 3).reshape(replicas, SUBLANES, width)
    n_x, n_lo = lax.axis_size("x"), lax.axis_size("z_lo")
    from_x, from_lo = PIECE_START
    along_x, along_lo = turned(n_x, from_x), turned(n_lo, from_lo)
    along_rep = [x * n_lo + z_lo for x in along_x for z_lo in along_lo]
    received = lax.all_to_all(pieces, REP, 0, 0, axis_index_groups=[along_rep], tiled=True)
    me = (lax.axis_index("x") + n_x - from_x) % n_x * n_lo + (lax.axis_index("z_lo") + n_lo - from_lo) % n_lo
    own = lax.dynamic_slice(master, (me // across * SUBLANES, me % across * width), (SUBLANES, width))
    mean = jnp.sum(own[None] - received.astype(jnp.float32), axis=0) / replicas
    kept = 0.9 * momentum
    base = master - 0.63 * kept
    mean, kept, base = lax.optimization_barrier((mean, kept, base))
    coded = encode(mean)
    near = replicas // bands
    copies = jnp.broadcast_to(coded[None], (near,) + coded.shape)
    firsts = [along_rep[start : start + near] for start in range(0, replicas, near)]
    band = lax.all_to_all(copies, REP, 0, 0, axis_index_groups=firsts, tiled=True)
    seconds = [[along_x[step], along_x[n_x - 1 - step]] for step in range(bands)]
    groups = near_groups(seconds)
    members = len(groups[0])
    vmem = pl.BlockSpec(memory_space=pltpu.VMEM)
    shares = pl.pallas_call(
        squares_kernel,
        out_shape=jax.ShapeDtypeStruct((members, LANES), jnp.float32),
        in_specs=[vmem],
        out_specs=vmem,
        compiler_params=pltpu.CompilerParams(vmem_limit_bytes=4 << 20),
        cost_estimate=pl.CostEstimate(flops=3 * band.size, bytes_accessed=4 * band.size, transcendentals=0),
    )(band.astype(jnp.float32))
    shares = lax.all_to_all(shares.reshape(members, 1, LANES), NAMES, 0, 0, axis_index_groups=groups, tiled=True)
    gathered = lax.all_gather(band, "x", axis_index_groups=seconds).reshape(replicas, SUBLANES, width + LANES).astype(jnp.float32)
    whole = jax.ShapeDtypeStruct((rows, cols), jnp.float32)
    half = jax.ShapeDtypeStruct((rows, cols), jnp.bfloat16)
    hbm = pl.BlockSpec(memory_space=pl.ANY)
    return pl.pallas_call(
        lambda *refs: finish_kernel(element_count, *refs),
        out_shape=(whole, whole, half),
        in_specs=[vmem] * 4,
        out_specs=(hbm,) * 3,
        scratch_shapes=[
            pltpu.VMEM((rows, cols), jnp.float32),
            pltpu.VMEM((rows, cols), jnp.float32),
            pltpu.VMEM((rows, cols), jnp.bfloat16),
            pltpu.SemaphoreType.DMA((3, OUT_CHUNKS)),
        ],
        compiler_params=pltpu.CompilerParams(vmem_limit_bytes=16 << 20),
        cost_estimate=pl.CostEstimate(flops=8 * rows * cols, bytes_accessed=22 * rows * cols, transcendentals=0),
    )(shares.reshape(members, LANES), gathered, kept, base)


def solution(mesh):
    fine = Mesh(mesh.devices.reshape(SIZES), NAMES)
    rows = P(FSDP, None)
    return jax.shard_map(
        shards,
        mesh=fine,
        in_specs=(P(REP, FSDP, None), rows, rows),
        out_specs=(rows, rows, rows),
        check_vma=False,
    )
```

```python
import math

import jax
import jax.numpy as jnp
from jax import lax
from jax.experimental import pallas as pl
from jax.experimental.pallas import tpu as pltpu
from jax.sharding import Mesh, PartitionSpec as P

SIZES = (4, 4, 4, 4, 2)
NAMES = ("x", "z_lo", "y", "z_hi", "core")
REP = ("x", "z_lo")
FSDP = ("y", "z_hi", "core")
LANES = 128
SUBLANES = 8
OUT_CHUNKS = 4
PIECE_START = (3, 2)
SHARE_START = (2, 3)
TOP = 14
FLOOR = 2.0**-100


def turned(size, start):
    return [(start + step) % size for step in range(size)]


def position(x, z_lo, y, z_hi, core):
    place = 0
    for size, index in zip(SIZES, (x, z_lo, y, z_hi, core)):
        place = place * size + index
    return place


def near_groups(pairs):
    n_x, n_lo, n_y, n_hi, n_core = SIZES
    from_y, from_hi = SHARE_START
    return [
        [
            position(x, (z_lo + n_lo // 2 * (z_hi * 2 // n_hi)) % n_lo, y, z_hi, core)
            for x in sorted(pair)
            for y in turned(n_y, from_y)
            for z_hi in turned(n_hi, from_hi)
            for core in range(n_core)
        ]
        for pair in pairs
        for z_lo in range(n_lo)
    ]


def blocks(width):
    return [slice(start, start + LANES) for start in range(0, width, LANES)]


def encode(piece):
    parts = [piece[:, at] for at in blocks(piece.shape[1])]
    largest = jnp.full_like(parts[0], FLOOR)
    for part in parts:
        largest = jnp.maximum(largest, jnp.abs(part))
    exponent = jnp.ceil(jnp.log2(largest))
    power = jnp.exp2(TOP - exponent)
    return jnp.concatenate([part * power for part in parts] + [exponent], axis=1).astype(jnp.float16)


def power_of(coded_ref, piece, width):
    return jnp.exp2(coded_ref[piece, :, width : width + LANES] - TOP)


def squares_kernel(coded_ref, shares_ref):
    pieces, _, coded_width = coded_ref.shape
    width = coded_width - LANES
    total = jnp.zeros((SUBLANES, LANES), jnp.float32)
    for piece in range(pieces):
        power = power_of(coded_ref, piece, width)
        for at in blocks(width):
            value = coded_ref[piece, :, at] * power
            total = total + value * value
    lanes = jnp.sum(total, axis=0, keepdims=True)
    shares_ref[...] = jnp.broadcast_to(lanes, shares_ref.shape)


def finish_kernel(
    element_count, shares_ref, coded_ref, kept_ref, base_ref,
    new_master_ref, new_momentum_ref, working_ref,
    master_slot, momentum_slot, working_slot, sems,
):
    pieces, _, coded_width = coded_ref.shape
    width = coded_width - LANES
    rows, cols = kept_ref.shape
    bands = rows // SUBLANES
    across = pieces // bands
    half = shares_ref.shape[0] // 2
    squares = jnp.sum(shares_ref[:half], keepdims=True) + jnp.sum(shares_ref[half:], keepdims=True)
    factor = jnp.minimum(1.0, 0.5 * math.sqrt(element_count) * lax.rsqrt(squares + 1e-06))
    copies = []
    chunk = cols // OUT_CHUNKS
    for block in range(across):
        own = [band * across + block for band in range(bands)]
        powers = [power_of(coded_ref, piece, width) for piece in own]
        for part in blocks(width):
            at = slice(block * width + part.start, block * width + part.stop)
            pseudo = jnp.concatenate([coded_ref[piece, :, part] * power for piece, power in zip(own, powers)], axis=0)
            clipped = factor * pseudo
            new_momentum = kept_ref[:, at] + clipped
            new_master = base_ref[:, at] - 1.33 * clipped
            momentum_slot[:, at] = new_momentum
            master_slot[:, at] = new_master
            working_slot[:, at] = new_master.astype(jnp.bfloat16)
        done = (block + 1) * width
        if done % chunk == 0:
            part = slice(done - chunk, done)
            pairs = ((master_slot, new_master_ref), (momentum_slot, new_momentum_ref), (working_slot, working_ref))
            for k, (slot, out) in enumerate(pairs):
                copy = pltpu.make_async_copy(slot.at[:, part], out.at[:, part], sems.at[k, done // chunk - 1])
                copy.start()
                copies.append(copy)
    for copy in copies:
        copy.wait()


def shards(inner_weights, master, momentum):
    replicas = lax.axis_size(REP)
    rows, cols = master.shape
    element_count = rows * lax.axis_size(FSDP) * cols
    bands = rows // SUBLANES
    across = replicas // bands
    width = cols // across
    pieces = inner_weights[0].reshape(bands, SUBLANES, across, width).transpose(0, 2, 1, 3).reshape(replicas, SUBLANES, width)
    n_x, n_lo = lax.axis_size("x"), lax.axis_size("z_lo")
    from_x, from_lo = PIECE_START
    along_x, along_lo = turned(n_x, from_x), turned(n_lo, from_lo)
    along_rep = [x * n_lo + z_lo for x in along_x for z_lo in along_lo]
    received = lax.all_to_all(pieces, REP, 0, 0, axis_index_groups=[along_rep], tiled=True)
    me = (lax.axis_index("x") + n_x - from_x) % n_x * n_lo + (lax.axis_index("z_lo") + n_lo - from_lo) % n_lo
    own = lax.dynamic_slice(master, (me // across * SUBLANES, me % across * width), (SUBLANES, width))
    mean = jnp.sum(own[None] - received.astype(jnp.float32), axis=0) / replicas
    kept = 0.9 * momentum
    base = master - 0.63 * kept
    mean, kept, base = lax.optimization_barrier((mean, kept, base))
    coded = encode(mean)
    near = replicas // bands
    copies = jnp.broadcast_to(coded[None], (near,) + coded.shape)
    firsts = [along_rep[start : start + near] for start in range(0, replicas, near)]
    band = lax.all_to_all(copies, REP, 0, 0, axis_index_groups=firsts, tiled=True)
    seconds = [[along_x[step], along_x[n_x - 1 - step]] for step in range(bands)]
    groups = near_groups(seconds)
    members = len(groups[0])
    vmem = pl.BlockSpec(memory_space=pltpu.VMEM)
    shares = pl.pallas_call(
        squares_kernel,
        out_shape=jax.ShapeDtypeStruct((members, LANES), jnp.float32),
        in_specs=[vmem],
        out_specs=vmem,
        compiler_params=pltpu.CompilerParams(vmem_limit_bytes=4 << 20),
        cost_estimate=pl.CostEstimate(flops=3 * band.size, bytes_accessed=4 * band.size, transcendentals=0),
    )(band.astype(jnp.float32))
    shares = lax.all_to_all(shares.reshape(members, 1, LANES), NAMES, 0, 0, axis_index_groups=groups, tiled=True)
    gathered = lax.all_gather(band, "x", axis_index_groups=seconds).reshape(replicas, SUBLANES, width + LANES).astype(jnp.float32)
    whole = jax.ShapeDtypeStruct((rows, cols), jnp.float32)
    half = jax.ShapeDtypeStruct((rows, cols), jnp.bfloat16)
    hbm = pl.BlockSpec(memory_space=pl.ANY)
    return pl.pallas_call(
        lambda *refs: finish_kernel(element_count, *refs),
        out_shape=(whole, whole, half),
        in_specs=[vmem] * 4,
        out_specs=(hbm,) * 3,
        scratch_shapes=[
            pltpu.VMEM((rows, cols), jnp.float32),
            pltpu.VMEM((rows, cols), jnp.float32),
            pltpu.VMEM((rows, cols), jnp.bfloat16),
            pltpu.SemaphoreType.DMA((3, OUT_CHUNKS)),
        ],
        compiler_params=pltpu.CompilerParams(vmem_limit_bytes=16 << 20),
        cost_estimate=pl.CostEstimate(flops=8 * rows * cols, bytes_accessed=22 * rows * cols, transcendentals=0),
    )(shares.reshape(members, LANES), gathered, kept, base)


def solution(mesh):
    fine = Mesh(mesh.devices.reshape(SIZES), NAMES)
    rows = P(FSDP, None)
    return jax.shard_map(
        shards,
        mesh=fine,
        in_specs=(P(REP, FSDP, None), rows, rows),
        out_specs=(rows, rows, rows),
        check_vma=False,
    )
```

```python
import math

import jax
import jax.numpy as jnp
from jax import lax
from jax.experimental import pallas as pl
from jax.experimental.pallas import tpu as pltpu
from jax.sharding import Mesh, PartitionSpec as P

SIZES = (4, 4, 4, 4, 2)
NAMES = ("x", "z_lo", "y", "z_hi", "core")
REP = ("x", "z_lo")
FSDP = ("y", "z_hi", "core")
LANES = 128
SUBLANES = 8
OUT_CHUNKS = 4
PIECE_START = (3, 2)
SHARE_START = (2, 3)
TOP = 14
FLOOR = 2.0**-100


def turned(size, start):
    return [(start + step) % size for step in range(size)]


def position(x, z_lo, y, z_hi, core):
    place = 0
    for size, index in zip(SIZES, (x, z_lo, y, z_hi, core)):
        place = place * size + index
    return place


def near_groups(pairs):
    n_x, n_lo, n_y, n_hi, n_core = SIZES
    from_y, from_hi = SHARE_START
    return [
        [
            position(x, (z_lo + n_lo // 2 * (z_hi * 2 // n_hi)) % n_lo, y, z_hi, core)
            for x in pair
            for y in turned(n_y, from_y)
            for z_hi in turned(n_hi, from_hi)
            for core in range(n_core)
        ]
        for pair in pairs
        for z_lo in range(n_lo)
    ]


def blocks(width):
    return [slice(start, start + LANES) for start in range(0, width, LANES)]


def encode(piece):
    parts = [piece[:, at] for at in blocks(piece.shape[1])]
    largest = jnp.full_like(parts[0], FLOOR)
    for part in parts:
        largest = jnp.maximum(largest, jnp.abs(part))
    exponent = jnp.ceil(jnp.log2(largest))
    power = jnp.exp2(TOP - exponent)
    return jnp.concatenate([part * power for part in parts] + [exponent], axis=1).astype(jnp.float16)


def power_of(coded_ref, piece, width):
    return jnp.exp2(coded_ref[piece, :, width : width + LANES] - TOP)


def squares_kernel(coded_ref, shares_ref):
    pieces, _, coded_width = coded_ref.shape
    width = coded_width - LANES
    total = jnp.zeros((SUBLANES, LANES), jnp.float32)
    for piece in range(pieces):
        power = power_of(coded_ref, piece, width)
        for at in blocks(width):
            value = coded_ref[piece, :, at] * power
            total = total + value * value
    lanes = jnp.sum(total, axis=0, keepdims=True)
    shares_ref[...] = jnp.broadcast_to(lanes, shares_ref.shape)


def finish_kernel(
    element_count, shares_ref, coded_ref, kept_ref, base_ref,
    new_master_ref, new_momentum_ref, working_ref,
    master_slot, momentum_slot, working_slot, sems,
):
    pieces, _, coded_width = coded_ref.shape
    width = coded_width - LANES
    rows, cols = kept_ref.shape
    bands = rows // SUBLANES
    across = pieces // bands
    half = shares_ref.shape[0] // 2
    squares = jnp.sum(shares_ref[:half], keepdims=True) + jnp.sum(shares_ref[half:], keepdims=True)
    factor = jnp.minimum(1.0, 0.5 * math.sqrt(element_count) * lax.rsqrt(squares + 1e-06))
    copies = []
    chunk = cols // OUT_CHUNKS
    for block in range(across):
        own = [band * across + block for band in range(bands)]
        powers = [power_of(coded_ref, piece, width) for piece in own]
        for part in blocks(width):
            at = slice(block * width + part.start, block * width + part.stop)
            pseudo = jnp.concatenate([coded_ref[piece, :, part] * power for piece, power in zip(own, powers)], axis=0)
            clipped = factor * pseudo
            new_momentum = kept_ref[:, at] + clipped
            new_master = base_ref[:, at] - 1.33 * clipped
            momentum_slot[:, at] = new_momentum
            master_slot[:, at] = new_master
            working_slot[:, at] = new_master.astype(jnp.bfloat16)
        done = (block + 1) * width
        if done % chunk == 0:
            part = slice(done - chunk, done)
            pairs = ((master_slot, new_master_ref), (momentum_slot, new_momentum_ref), (working_slot, working_ref))
            for k, (slot, out) in enumerate(pairs):
                copy = pltpu.make_async_copy(slot.at[:, part], out.at[:, part], sems.at[k, done // chunk - 1])
                copy.start()
                copies.append(copy)
    for copy in copies:
        copy.wait()


def shards(inner_weights, master, momentum):
    replicas = lax.axis_size(REP)
    rows, cols = master.shape
    element_count = rows * lax.axis_size(FSDP) * cols
    bands = rows // SUBLANES
    across = replicas // bands
    width = cols // across
    pieces = inner_weights[0].reshape(bands, SUBLANES, across, width).transpose(0, 2, 1, 3).reshape(replicas, SUBLANES, width)
    n_x, n_lo = lax.axis_size("x"), lax.axis_size("z_lo")
    from_x, from_lo = PIECE_START
    along_x, along_lo = turned(n_x, from_x), turned(n_lo, from_lo)
    along_rep = [x * n_lo + z_lo for x in along_x for z_lo in along_lo]
    received = lax.all_to_all(pieces, REP, 0, 0, axis_index_groups=[along_rep], tiled=True)
    me = (lax.axis_index("x") + n_x - from_x) % n_x * n_lo + (lax.axis_index("z_lo") + n_lo - from_lo) % n_lo
    own = lax.dynamic_slice(master, (me // across * SUBLANES, me % across * width), (SUBLANES, width))
    mean = jnp.sum(own[None] - received.astype(jnp.float32), axis=0) / replicas
    kept = 0.9 * momentum
    base = master - 0.63 * kept
    mean, kept, base = lax.optimization_barrier((mean, kept, base))
    coded = encode(mean)
    near = replicas // bands
    copies = jnp.broadcast_to(coded[None], (near,) + coded.shape)
    firsts = [along_rep[start : start + near] for start in range(0, replicas, near)]
    band = lax.all_to_all(copies, REP, 0, 0, axis_index_groups=firsts, tiled=True)
    seconds = [[along_x[step], along_x[n_x - 1 - step]] for step in range(bands)]
    groups = near_groups(seconds)
    members = len(groups[0])
    vmem = pl.BlockSpec(memory_space=pltpu.VMEM)
    shares = pl.pallas_call(
        squares_kernel,
        out_shape=jax.ShapeDtypeStruct((members, LANES), jnp.float32),
        in_specs=[vmem],
        out_specs=vmem,
        compiler_params=pltpu.CompilerParams(vmem_limit_bytes=4 << 20),
        cost_estimate=pl.CostEstimate(flops=3 * band.size, bytes_accessed=4 * band.size, transcendentals=0),
    )(band.astype(jnp.float32))
    shares = lax.all_to_all(shares.reshape(members, 1, LANES), NAMES, 0, 0, axis_index_groups=groups, tiled=True)
    gathered = lax.all_gather(band, "x", axis_index_groups=seconds).reshape(replicas, SUBLANES, width + LANES).astype(jnp.float32)
    whole = jax.ShapeDtypeStruct((rows, cols), jnp.float32)
    half = jax.ShapeDtypeStruct((rows, cols), jnp.bfloat16)
    hbm = pl.BlockSpec(memory_space=pl.ANY)
    return pl.pallas_call(
        lambda *refs: finish_kernel(element_count, *refs),
        out_shape=(whole, whole, half),
        in_specs=[vmem] * 4,
        out_specs=(hbm,) * 3,
        scratch_shapes=[
            pltpu.VMEM((rows, cols), jnp.float32),
            pltpu.VMEM((rows, cols), jnp.float32),
            pltpu.VMEM((rows, cols), jnp.bfloat16),
            pltpu.SemaphoreType.DMA((3, OUT_CHUNKS)),
        ],
        compiler_params=pltpu.CompilerParams(vmem_limit_bytes=16 << 20),
        cost_estimate=pl.CostEstimate(flops=8 * rows * cols, bytes_accessed=22 * rows * cols, transcendentals=0),
    )(shares.reshape(members, LANES), gathered, kept, base)


def solution(mesh):
    fine = Mesh(mesh.devices.reshape(SIZES), NAMES)
    rows = P(FSDP, None)
    return jax.shard_map(
        shards,
        mesh=fine,
        in_specs=(P(REP, FSDP, None), rows, rows),
        out_specs=(rows, rows, rows),
        check_vma=False,
    )
```

```python
import math

import jax
import jax.numpy as jnp
from jax import lax
from jax.experimental import pallas as pl
from jax.experimental.pallas import tpu as pltpu
from jax.sharding import Mesh, PartitionSpec as P

SIZES = (4, 4, 4, 4, 2)
NAMES = ("x", "z_lo", "y", "z_hi", "core")
REP = ("x", "z_lo")
FSDP = ("y", "z_hi", "core")
LANES = 128
SUBLANES = 8
OUT_CHUNKS = 8
PIECE_START = (3, 2)
SHARE_START = (2, 3)
TOP = 14
FLOOR = 2.0**-100


def turned(size, start):
    return [(start + step) % size for step in range(size)]


def position(x, z_lo, y, z_hi, core):
    place = 0
    for size, index in zip(SIZES, (x, z_lo, y, z_hi, core)):
        place = place * size + index
    return place


def near_groups(pairs):
    n_x, n_lo, n_y, n_hi, n_core = SIZES
    from_y, from_hi = SHARE_START
    return [
        [
            position(x, (z_lo + n_lo // 2 * (z_hi * 2 // n_hi)) % n_lo, y, z_hi, core)
            for x in sorted(pair)
            for y in turned(n_y, from_y)
            for z_hi in turned(n_hi, from_hi)
            for core in range(n_core)
        ]
        for pair in pairs
        for z_lo in range(n_lo)
    ]


def blocks(width):
    return [slice(start, start + LANES) for start in range(0, width, LANES)]


def encode(piece):
    parts = [piece[:, at] for at in blocks(piece.shape[1])]
    largest = jnp.full_like(parts[0], FLOOR)
    for part in parts:
        largest = jnp.maximum(largest, jnp.abs(part))
    exponent = jnp.ceil(jnp.log2(largest))
    power = jnp.exp2(TOP - exponent)
    return jnp.concatenate([part * power for part in parts] + [exponent], axis=1).astype(jnp.float16)


def power_of(coded_ref, piece, width):
    return jnp.exp2(coded_ref[piece, :, width : width + LANES] - TOP)


def squares_kernel(coded_ref, shares_ref):
    pieces, _, coded_width = coded_ref.shape
    width = coded_width - LANES
    total = jnp.zeros((SUBLANES, LANES), jnp.float32)
    for piece in range(pieces):
        power = power_of(coded_ref, piece, width)
        for at in blocks(width):
            value = coded_ref[piece, :, at] * power
            total = total + value * value
    lanes = jnp.sum(total, axis=0, keepdims=True)
    shares_ref[...] = jnp.broadcast_to(lanes, shares_ref.shape)


def finish_kernel(
    element_count, shares_ref, coded_ref, kept_ref, base_ref,
    new_master_ref, new_momentum_ref, working_ref,
    master_slot, momentum_slot, working_slot, sems,
):
    pieces, _, coded_width = coded_ref.shape
    width = coded_width - LANES
    rows, cols = kept_ref.shape
    bands = rows // SUBLANES
    across = pieces // bands
    half = shares_ref.shape[0] // 2
    squares = jnp.sum(shares_ref[:half], keepdims=True) + jnp.sum(shares_ref[half:], keepdims=True)
    factor = jnp.minimum(1.0, 0.5 * math.sqrt(element_count) * lax.rsqrt(squares + 1e-06))
    copies = []
    chunk = cols // OUT_CHUNKS
    for block in range(across):
        own = [band * across + block for band in range(bands)]
        powers = [power_of(coded_ref, piece, width) for piece in own]
        for part in blocks(width):
            at = slice(block * width + part.start, block * width + part.stop)
            pseudo = jnp.concatenate([coded_ref[piece, :, part] * power for piece, power in zip(own, powers)], axis=0)
            clipped = factor * pseudo
            new_momentum = kept_ref[:, at] + clipped
            new_master = base_ref[:, at] - 1.33 * clipped
            momentum_slot[:, at] = new_momentum
            master_slot[:, at] = new_master
            working_slot[:, at] = new_master.astype(jnp.bfloat16)
        done = (block + 1) * width
        if done % chunk == 0:
            part = slice(done - chunk, done)
            pairs = ((master_slot, new_master_ref), (momentum_slot, new_momentum_ref), (working_slot, working_ref))
            for k, (slot, out) in enumerate(pairs):
                copy = pltpu.make_async_copy(slot.at[:, part], out.at[:, part], sems.at[k, done // chunk - 1])
                copy.start()
                copies.append(copy)
    for copy in copies:
        copy.wait()


def shards(inner_weights, master, momentum):
    replicas = lax.axis_size(REP)
    rows, cols = master.shape
    element_count = rows * lax.axis_size(FSDP) * cols
    bands = rows // SUBLANES
    across = replicas // bands
    width = cols // across
    pieces = inner_weights[0].reshape(bands, SUBLANES, across, width).transpose(0, 2, 1, 3).reshape(replicas, SUBLANES, width)
    n_x, n_lo = lax.axis_size("x"), lax.axis_size("z_lo")
    from_x, from_lo = PIECE_START
    along_x, along_lo = turned(n_x, from_x), turned(n_lo, from_lo)
    along_rep = [x * n_lo + z_lo for x in along_x for z_lo in along_lo]
    received = lax.all_to_all(pieces, REP, 0, 0, axis_index_groups=[along_rep], tiled=True)
    me = (lax.axis_index("x") + n_x - from_x) % n_x * n_lo + (lax.axis_index("z_lo") + n_lo - from_lo) % n_lo
    own = lax.dynamic_slice(master, (me // across * SUBLANES, me % across * width), (SUBLANES, width))
    mean = jnp.sum(own[None] - received.astype(jnp.float32), axis=0) / replicas
    kept = 0.9 * momentum
    base = master - 0.63 * kept
    mean, kept, base = lax.optimization_barrier((mean, kept, base))
    coded = encode(mean)
    near = replicas // bands
    copies = jnp.broadcast_to(coded[None], (near,) + coded.shape)
    firsts = [along_rep[start : start + near] for start in range(0, replicas, near)]
    band = lax.all_to_all(copies, REP, 0, 0, axis_index_groups=firsts, tiled=True)
    seconds = [[along_x[step], along_x[n_x - 1 - step]] for step in range(bands)]
    groups = near_groups(seconds)
    members = len(groups[0])
    vmem = pl.BlockSpec(memory_space=pltpu.VMEM)
    shares = pl.pallas_call(
        squares_kernel,
        out_shape=jax.ShapeDtypeStruct((members, LANES), jnp.float32),
        in_specs=[vmem],
        out_specs=vmem,
        compiler_params=pltpu.CompilerParams(vmem_limit_bytes=4 << 20),
        cost_estimate=pl.CostEstimate(flops=3 * band.size, bytes_accessed=4 * band.size, transcendentals=0),
    )(band.astype(jnp.float32))
    shares = lax.all_to_all(shares.reshape(members, 1, LANES), NAMES, 0, 0, axis_index_groups=groups, tiled=True)
    gathered = lax.all_gather(band, "x", axis_index_groups=seconds).reshape(replicas, SUBLANES, width + LANES).astype(jnp.float32)
    whole = jax.ShapeDtypeStruct((rows, cols), jnp.float32)
    half = jax.ShapeDtypeStruct((rows, cols), jnp.bfloat16)
    hbm = pl.BlockSpec(memory_space=pl.ANY)
    return pl.pallas_call(
        lambda *refs: finish_kernel(element_count, *refs),
        out_shape=(whole, whole, half),
        in_specs=[vmem] * 4,
        out_specs=(hbm,) * 3,
        scratch_shapes=[
            pltpu.VMEM((rows, cols), jnp.float32),
            pltpu.VMEM((rows, cols), jnp.float32),
            pltpu.VMEM((rows, cols), jnp.bfloat16),
            pltpu.SemaphoreType.DMA((3, OUT_CHUNKS)),
        ],
        compiler_params=pltpu.CompilerParams(vmem_limit_bytes=16 << 20),
        cost_estimate=pl.CostEstimate(flops=8 * rows * cols, bytes_accessed=22 * rows * cols, transcendentals=0),
    )(shares.reshape(members, LANES), gathered, kept, base)


def solution(mesh):
    fine = Mesh(mesh.devices.reshape(SIZES), NAMES)
    rows = P(FSDP, None)
    return jax.shard_map(
        shards,
        mesh=fine,
        in_specs=(P(REP, FSDP, None), rows, rows),
        out_specs=(rows, rows, rows),
        check_vma=False,
    )
```
